32 devices in a mesh: seq: 16 (over z, y, x), chan: 2 (over core).
Axes of the slice: x: 2, y: 2, z: 4, core: 2. Of those that a mesh axis runs over, the one named last changes fastest.
Arguments:
- query_in: bfloat16 [8192, 4096], P('seq', 'chan'), may hold values from -6 to 6
- key_in: bfloat16 [8192, 4096], P('seq', 'chan'), may hold values from -6 to 6
- value_in: bfloat16 [8192, 4096], P('seq', 'chan'), may hold values from -6 to 6
- decay_time: float32 [4096, 16], P('chan'), may hold values from 30 to 32768
- residue: float32 [4096, 16], P('chan'), may hold values from -27 to 27
- out_weight: bfloat16 [4096, 4096], P('chan'), may hold values from -0.09375 to 0.09375
- cotangent: bfloat16 [8192, 4096], P('seq', 'chan'), may hold values from -6 to 6
Outputs:
- mixed_out: bfloat16 [8192, 4096], P('seq', 'chan')
- query_grad: bfloat16 [8192, 4096], P('seq', 'chan')
- key_grad: bfloat16 [8192, 4096], P('seq', 'chan')
- value_grad: bfloat16 [8192, 4096], P('seq', 'chan')
- residue_grad: float32 [4096, 16], P('chan')
The draws below stay inside these ranges and needn't reach their ends.
All inputs are finite; a program needn't handle non-finite values.
Results may differ from the reference program's by a relative error of at most 0.02.
Values may be sent and summed in bfloat16 or wider, within the bound.
A program may use at most 192 MiB of HBM per device.

```python
import math
import jax
import jax.numpy as jnp
from jax import lax

CHANNELS = 4096
MODES = 16
TOKENS = 8192
N_CHAN = 2


def modal_groups(key, slow_share):
    base_key = jax.random.fold_in(key, 7001)
    kind_key, slow_key, quick_key, size_key, sign_key, mix_key, free_key = jax.random.split(base_key, 7)
    group_count = MODES // 4
    spacing = 0.5
    group_span = 3.0 * spacing
    is_slow = jax.random.uniform(kind_key, (CHANNELS, group_count), jnp.float32) < slow_share
    slow_fastest = jnp.exp(jax.random.uniform(slow_key, (CHANNELS, group_count), jnp.float32, math.log(TOKENS / 8.0), math.log(4.0 * TOKENS) - group_span))
    quick_fastest = jnp.exp(jax.random.uniform(quick_key, (CHANNELS, group_count), jnp.float32, math.log(30.0), math.log(max(40.0, TOKENS / 36.0))))
    fastest = jnp.where(is_slow, slow_fastest, quick_fastest)
    offsets = spacing * (3.0 - jnp.arange(4, dtype=jnp.float32))
    time_table = fastest[:, :, None] * jnp.exp(offsets)[None, None, :]
    decay_time = jnp.clip(time_table.reshape(CHANNELS, MODES), 30.0, 4.0 * TOKENS)
    amplitude = jnp.exp(jax.random.uniform(size_key, (CHANNELS, group_count), jnp.float32, 0.0, math.log(3.0)))
    amplitude = amplitude * jnp.where(is_slow, 3.0, 1.5)
    sign_flip = jnp.where(jax.random.uniform(sign_key, (CHANNELS, group_count), jnp.float32) < 0.5, -1.0, 1.0)
    pattern = jnp.array([1.0, -3.0, 3.0, -1.0], jnp.float32)
    structured = (sign_flip * amplitude)[:, :, None] * pattern[None, None, :]
    free_part = jnp.clip(0.25 * jax.random.normal(free_key, (CHANNELS, group_count, 4), jnp.float32), -1.5, 1.5)
    is_free = jax.random.uniform(mix_key, (CHANNELS, group_count), jnp.float32) < 0.25
    residue = jnp.where(is_free[:, :, None], free_part, structured).reshape(CHANNELS, MODES)
    residue = jnp.clip(residue, -27.0, 27.0)
    return (decay_time.astype(jnp.float32), residue.astype(jnp.float32))


def draw_decay_time(key, part):
    slow_share = 0.5
    return modal_groups(key, slow_share)[0]


def draw_residue(key, part):
    slow_share = 0.5
    return modal_groups(key, slow_share)[1]


def block_levels(key, shape, pieces, smallest, top_value):
    def one(position, parts):
        steps = jax.random.uniform(jax.random.fold_in(jax.random.fold_in(key, 6), position), (parts,), jnp.float32, smallest / len(pieces), top_value / len(pieces))
        return jnp.repeat(jnp.exp(steps), shape[position] // parts).reshape((-1,) + (1,) * (len(shape) - position - 1))

    gain = one(*pieces[0])
    for cut in pieces[1:]:
        gain = gain * one(*cut)
    return gain


def normal_values(own_key, shape, width, bound, pieces=(), kind=jnp.bfloat16):
    drawn = width * jax.random.normal(own_key, shape, jnp.float32)
    if pieces:
        drawn = drawn * block_levels(own_key, shape, pieces, -0.22, 0.18)
    return jnp.clip(drawn, -bound, bound).astype(kind)


def setup_inputs(seed: int = 0) -> dict:
    keys = jax.random.split(jax.random.key(seed), 8)
    query_in = normal_values(keys[0], (TOKENS, CHANNELS), 1.0, 6.0, ((0, 16), (1, 2)))
    key_in = normal_values(keys[1], (TOKENS, CHANNELS), 1.0, 6.0, ((0, 16), (1, 2)))
    value_in = normal_values(keys[2], (TOKENS, CHANNELS), 1.0, 6.0, ((0, 16), (1, 2)))
    decay_time = draw_decay_time(jax.random.fold_in(keys[7], 71), 0)
    residue = draw_residue(jax.random.fold_in(keys[7], 71), 0)
    out_weight = normal_values(keys[5], (CHANNELS, CHANNELS), CHANNELS ** -0.5, 0.09375, ((0, 2),))
    cotangent = normal_values(keys[6], (TOKENS, CHANNELS), 1.0, 6.0, ((0, 16), (1, 2)))
    return dict(query_in=query_in, key_in=key_in, value_in=value_in, decay_time=decay_time, residue=residue, out_weight=out_weight, cotangent=cotangent)


def reference(query_in, key_in, value_in, decay_time, residue, out_weight, cotangent):
    decay_rate = 1.0 / decay_time
    decay_step = jnp.exp(-decay_rate)
    norm_factor = jnp.sqrt(-jnp.expm1(-2.0 * decay_rate))
    mode_gain = norm_factor * residue
    product = (key_in.astype(jnp.float32) * value_in.astype(jnp.float32)).astype(jnp.bfloat16)
    grad_gated = jnp.dot(cotangent, out_weight.T, preferred_element_type=jnp.float32)
    weighted = (grad_gated * query_in.astype(jnp.float32)).astype(jnp.bfloat16)
    empty_modes = jnp.zeros(decay_step.shape, jnp.float32)

    def forward(carried, inputs):
        modal, correlation = carried
        product_row, weighted_row = inputs
        modal = decay_step * modal + product_row.astype(jnp.float32)[:, None]
        correlation = correlation + weighted_row.astype(jnp.float32)[:, None] * modal
        return ((modal, correlation), lax.optimization_barrier(jnp.sum(mode_gain * modal, axis=1)))
    (modal_end, correlation), convolved = lax.scan(forward, (empty_modes, empty_modes), (product, weighted))

    def backward(modal, weighted_row):
        modal = decay_step * modal + weighted_row.astype(jnp.float32)[:, None]
        return (modal, lax.optimization_barrier(jnp.sum(mode_gain * modal, axis=1)))
    back_end, grad_product = lax.scan(backward, empty_modes, weighted, reverse=True)
    gated = (query_in.astype(jnp.float32) * convolved).astype(jnp.bfloat16)
    group_size = CHANNELS // N_CHAN
    summed = jnp.zeros((TOKENS, CHANNELS), jnp.float32)
    for group_index in range(N_CHAN):
        first = group_index * group_size
        rounded_part = jnp.dot(gated[:, first:first + group_size], out_weight[first:first + group_size], preferred_element_type=jnp.float32).astype(jnp.bfloat16)
        summed = summed + lax.optimization_barrier(rounded_part).astype(jnp.float32)
    mixed_out = summed.astype(jnp.bfloat16)
    query_grad = (grad_gated * convolved).astype(jnp.bfloat16)
    key_grad = (grad_product * value_in.astype(jnp.float32)).astype(jnp.bfloat16)
    value_grad = (grad_product * key_in.astype(jnp.float32)).astype(jnp.bfloat16)
    residue_grad = norm_factor * correlation / jnp.sqrt(jnp.float32(TOKENS))
    return (mixed_out, query_grad, key_grad, value_grad, residue_grad)
```

```python
import functools

import jax
import jax.numpy as jnp
from jax import lax
from jax.experimental import pallas as pl
from jax.experimental.pallas import tpu as pltpu
from jax.sharding import PartitionSpec as P

LANES = 128
BLOCKS = 8
UNROLL = 8
F32 = jnp.float32
BF16 = jnp.bfloat16


def tree_sum(terms):
    while len(terms) > 1:
        pairs = [terms[i] + terms[i + 1] for i in range(0, len(terms) - 1, 2)]
        terms = pairs + terms[len(terms) - len(terms) % 2 :]
    return terms[0]


def row(ref, t, steps):
    return ref[pl.ds(t, BLOCKS, stride=steps), :]


def spread_rows(rate, first, count):
    return [
        jnp.broadcast_to(rate[n : n + 1, :], (BLOCKS, LANES)) for n in range(first, first + count)
    ]


def run_states(source, decays, steps, backward):
    def body(outer, states):
        for inner in range(UNROLL):
            t = outer * UNROLL + inner
            x = row(source, steps - 1 - t if backward else t, steps)
            states = [d * s + x for d, s in zip(decays, states)]
        return states

    zeros = [jnp.zeros((BLOCKS, LANES), F32) for _ in decays]
    return lax.fori_loop(0, steps // UNROLL, body, zeros)


def join_blocks(ends, rate, steps, backward):
    modes = rate.shape[0]
    step_decay = jnp.exp(-rate * float(steps))
    total = jnp.zeros((modes, LANES), F32)
    for b in reversed(range(BLOCKS)) if backward else range(BLOCKS):
        total = total * step_decay + ends[pl.ds(b, modes, stride=BLOCKS), :]
    return total


def block_carries(gathered, ends, rate, place, steps, carries, backward):
    modes = rate.shape[0]
    count = gathered.shape[0]
    step_decay = jnp.exp(-rate * float(steps))
    device_decay = jnp.exp(-rate * float(steps * BLOCKS))
    run = jnp.zeros((modes, LANES), F32)
    for e in reversed(range(count)) if backward else range(count):
        kept = place < e if backward else place > e
        run = jnp.where(kept, run * device_decay + gathered[e], run)
    for b in reversed(range(BLOCKS)) if backward else range(BLOCKS):
        carries[pl.ds(b, modes, stride=BLOCKS), :] = run
        run = run * step_decay + ends[pl.ds(b, modes, stride=BLOCKS), :]


def forward_ends_kernel(key_ref, value_ref, rate_ref, ends_ref, total_ref, source):
    steps = key_ref.shape[0] // BLOCKS
    rate = rate_ref[...]
    modes = rate.shape[0]
    source[...] = (key_ref[...].astype(F32) * value_ref[...].astype(F32)).astype(BF16).astype(F32)
    decays = spread_rows(jnp.exp(-rate), 0, modes)
    for n, state in enumerate(run_states(source, decays, steps, False)):
        ends_ref[n * BLOCKS : (n + 1) * BLOCKS, :] = state
    total_ref[...] = join_blocks(ends_ref, rate, steps, False)


def backward_ends_kernel(grad_ref, query_ref, rate_ref, ends_ref, total_ref, source):
    steps = grad_ref.shape[0] // BLOCKS
    rate = rate_ref[...]
    modes = rate.shape[0]
    source[...] = (grad_ref[...] * query_ref[...].astype(F32)).astype(BF16).astype(F32)
    decays = spread_rows(jnp.exp(-rate), 0, modes)
    for n, state in enumerate(run_states(source, decays, steps, True)):
        ends_ref[n * BLOCKS : (n + 1) * BLOCKS, :] = state
    total_ref[...] = join_blocks(ends_ref, rate, steps, True)


def forward_kernel(
    place_ref,
    key_ref,
    value_ref,
    query_ref,
    grad_ref,
    rate_ref,
    gain_ref,
    ends_ref,
    gathered_ref,
    gated_ref,
    query_grad_ref,
    corr_ref,
    product,
    weighted,
    conv,
    carries,
):
    steps = key_ref.shape[0] // BLOCKS
    rate = rate_ref[...]
    modes = rate.shape[0]
    decay = jnp.exp(-rate)
    query = query_ref[...].astype(F32)
    product[...] = (key_ref[...].astype(F32) * value_ref[...].astype(F32)).astype(BF16).astype(F32)
    weighted[...] = (grad_ref[...] * query).astype(BF16).astype(F32)
    block_carries(gathered_ref, ends_ref, rate, place_ref[0], steps, carries, False)
    half = modes // 2
    for first in (0, half):
        decays = spread_rows(decay, first, half)
        gains = spread_rows(gain_ref[...], first, half)

        def body(outer, held, first=first, decays=decays, gains=gains):
            states, sums = held
            for inner in range(UNROLL):
                t = outer * UNROLL + inner
                x = row(product, t, steps)
                w = row(weighted, t, steps)
                states = [d * s + x for d, s in zip(decays, states)]
                sums = [c + w * s for c, s in zip(sums, states)]
                terms = [g * s for g, s in zip(gains, states)]
                if first:
                    terms.append(row(conv, t, steps))
                conv[pl.ds(t, BLOCKS, stride=steps), :] = tree_sum(terms)
            return states, sums

        starts = [carries[n * BLOCKS : (n + 1) * BLOCKS, :] for n in range(first, first + half)]
        zeros = [jnp.zeros((BLOCKS, LANES), F32) for _ in range(half)]
        _, sums = lax.fori_loop(0, steps // UNROLL, body, (starts, zeros))
        for n, total in enumerate(sums):
            corr_ref[first + n : first + n + 1, :] = jnp.sum(total, axis=0, keepdims=True)
    convolved = conv[...]
    gated_ref[...] = (query * convolved).astype(BF16)
    query_grad_ref[...] = (grad_ref[...] * convolved).astype(BF16)


def backward_kernel(
    place_ref,
    grad_ref,
    query_ref,
    key_ref,
    value_ref,
    rate_ref,
    gain_ref,
    ends_ref,
    gathered_ref,
    key_grad_ref,
    value_grad_ref,
    weighted,
    conv,
    carries,
):
    steps = key_ref.shape[0] // BLOCKS
    rate = rate_ref[...]
    modes = rate.shape[0]
    weighted[...] = (grad_ref[...] * query_ref[...].astype(F32)).astype(BF16).astype(F32)
    block_carries(gathered_ref, ends_ref, rate, place_ref[0], steps, carries, True)
    decays = spread_rows(jnp.exp(-rate), 0, modes)
    gains = spread_rows(gain_ref[...], 0, modes)

    def body(outer, states):
        for inner in range(UNROLL):
            t = steps - 1 - (outer * UNROLL + inner)
            x = row(weighted, t, steps)
            states = [d * s + x for d, s in zip(decays, states)]
            conv[pl.ds(t, BLOCKS, stride=steps), :] = tree_sum(
                [g * s for g, s in zip(gains, states)]
            )
        return states

    starts = [carries[n * BLOCKS : (n + 1) * BLOCKS, :] for n in range(modes)]
    lax.fori_loop(0, steps // UNROLL, body, starts)
    grad_product = conv[...]
    key_grad_ref[...] = (grad_product * value_ref[...].astype(F32)).astype(BF16)
    value_grad_ref[...] = (grad_product * key_ref[...].astype(F32)).astype(BF16)


def by_lanes(rows):
    return pl.BlockSpec((rows, LANES), lambda i: (0, i))


def call(kernel, arrays, specs, outs, scratch_rows, flops):
    width = outs[0].shape[1]
    moved = sum(a.size * a.dtype.itemsize for a in list(arrays) + list(outs))
    return pl.pallas_call(
        kernel,
        grid=(width // LANES,),
        in_specs=specs,
        out_specs=[by_lanes(o.shape[0]) for o in outs],
        out_shape=outs,
        scratch_shapes=[pltpu.VMEM((r, LANES), F32) for r in scratch_rows],
        cost_estimate=pl.CostEstimate(flops=flops, bytes_accessed=moved, transcendentals=0),
        compiler_params=pltpu.CompilerParams(vmem_limit_bytes=32 * 2**20),
    )(*arrays)


def per_device(query_in, key_in, value_in, decay_time, residue, out_weight, cotangent):
    decay_rate = 1.0 / decay_time
    norm_factor = jnp.sqrt(-jnp.expm1(-2.0 * decay_rate))
    rate = decay_rate.T
    gain = (norm_factor * residue).T
    seq_count = lax.axis_size("seq")
    place = lax.axis_index("seq").astype(jnp.int32).reshape(1)
    rows, width = query_in.shape
    modes = rate.shape[0]
    work = rows * width * modes
    ends_shape = jax.ShapeDtypeStruct((modes * BLOCKS, width), F32)
    total_shape = jax.ShapeDtypeStruct((modes, width), F32)
    wide = jax.ShapeDtypeStruct((rows, width), BF16)
    big, mode_spec, ends_spec = by_lanes(rows), by_lanes(modes), by_lanes(modes * BLOCKS)
    place_spec = pl.BlockSpec(memory_space=pltpu.SMEM)
    gathered_spec = pl.BlockSpec((seq_count, modes, LANES), lambda i: (0, 0, i))

    all_cotangent = lax.all_gather(cotangent, "chan", axis=1, tiled=True)
    forward_ends, forward_total = call(
        forward_ends_kernel,
        (key_in, value_in, rate),
        [big, big, mode_spec],
        [ends_shape, total_shape],
        [rows],
        2 * work,
    )
    forward_all = lax.all_gather(forward_total, "seq", axis=0)
    grad_gated = lax.dot_general(
        all_cotangent, out_weight, (((1,), (1,)), ((), ())), preferred_element_type=F32
    )
    backward_ends, backward_total = call(
        backward_ends_kernel,
        (grad_gated, query_in, rate),
        [big, big, mode_spec],
        [ends_shape, total_shape],
        [rows],
        2 * work,
    )
    backward_all = lax.all_gather(backward_total, "seq", axis=0)
    gated, query_grad, corr = call(
        forward_kernel,
        (place, key_in, value_in, query_in, grad_gated, rate, gain, forward_ends, forward_all),
        [place_spec, big, big, big, big, mode_spec, mode_spec, ends_spec, gathered_spec],
        [wide, wide, total_shape],
        [rows, rows, rows, modes * BLOCKS],
        6 * work,
    )
    partial_out = jnp.dot(gated, out_weight, preferred_element_type=F32)
    mixed_out = lax.psum_scatter(
        partial_out.astype(BF16), "chan", scatter_dimension=1, tiled=True
    )
    correlation = lax.psum(corr, "seq").T
    key_grad, value_grad = call(
        backward_kernel,
        (place, grad_gated, query_in, key_in, value_in, rate, gain, backward_ends, backward_all),
        [place_spec, big, big, big, big, mode_spec, mode_spec, ends_spec, gathered_spec],
        [wide, wide],
        [rows, rows, modes * BLOCKS],
        4 * work,
    )
    residue_grad = norm_factor * correlation / jnp.sqrt(F32(rows * seq_count))
    return (mixed_out, query_grad, key_grad, value_grad, residue_grad)


def solution(mesh):
    tokens, group = P("seq", "chan"), P("chan", None)
    return jax.shard_map(
        per_device,
        mesh=mesh,
        in_specs=(tokens, tokens, tokens, group, group, group, tokens),
        out_specs=(tokens, tokens, tokens, tokens, group),
        check_vma=False,
    )
```

```python
import functools

import jax
import jax.numpy as jnp
from jax import lax
from jax.experimental import pallas as pl
from jax.experimental.pallas import tpu as pltpu
from jax.sharding import PartitionSpec as P

LANES = 128
BLOCKS = 8
F32 = jnp.float32
BF16 = jnp.bfloat16


def tree_sum(terms):
    while len(terms) > 1:
        pairs = [terms[i] + terms[i + 1] for i in range(0, len(terms) - 1, 2)]
        terms = pairs + terms[len(terms) - len(terms) % 2 :]
    return terms[0]


def swap_rows(tiles):
    rows = lax.broadcasted_iota(jnp.int32, (BLOCKS, LANES), 0)
    for bit in (1, 2, 4):
        low = (rows & bit) == 0
        swapped = list(tiles)
        for i in range(BLOCKS):
            if i & bit == 0:
                a, b = tiles[i], tiles[i | bit]
                swapped[i] = jnp.where(low, a, pltpu.roll(b, bit, axis=0))
                swapped[i | bit] = jnp.where(low, pltpu.roll(a, BLOCKS - bit, axis=0), b)
        tiles = swapped
    return tiles


def block_tile(b, group, steps):
    return pl.ds(pl.multiple_of(b * steps + group * BLOCKS, BLOCKS), BLOCKS)


def load_steps(ref, group, steps):
    return swap_rows([ref[block_tile(b, group, steps), :] for b in range(BLOCKS)])


def store_steps(ref, group, steps, tiles):
    for b, tile in enumerate(swap_rows(tiles)):
        ref[block_tile(b, group, steps), :] = tile


def step_tile(group, inner):
    return pl.ds(pl.multiple_of((group * BLOCKS + inner) * BLOCKS, BLOCKS), BLOCKS)


def spread_rows(rate, first, count):
    return [
        jnp.broadcast_to(rate[n : n + 1, :], (BLOCKS, LANES)) for n in range(first, first + count)
    ]


def block_rows(ends, b, modes):
    return ends[pl.ds(b, modes, stride=BLOCKS), :]


def join_blocks(ends, rate, steps, backward):
    modes = rate.shape[0]
    step_decay = jnp.exp(-rate * float(steps))
    total = jnp.zeros((modes, LANES), F32)
    for b in reversed(range(BLOCKS)) if backward else range(BLOCKS):
        total = total * step_decay + block_rows(ends, b, modes)
    return total


def fill_carries(entering, ends, rate, steps, carries, backward):
    modes = rate.shape[0]
    step_decay = jnp.exp(-rate * float(steps))
    run = entering
    for b in reversed(range(BLOCKS)) if backward else range(BLOCKS):
        carries[pl.ds(b, modes, stride=BLOCKS), :] = run
        run = run * step_decay + block_rows(ends, b, modes)


def take(ref, n):
    return ref[n * BLOCKS : (n + 1) * BLOCKS, :]


def rounded_product(a, b):
    return (a.astype(F32) * b.astype(F32)).astype(BF16).astype(F32)


def zero_rows(count):
    return [jnp.zeros((BLOCKS, LANES), F32) for _ in range(count)]


def forward_local_kernel(
    key_ref, value_ref, rate_ref, gain_ref, conv_ref, ends_ref, total_ref, product
):
    steps = key_ref.shape[0] // BLOCKS
    rate = rate_ref[...]
    modes = rate.shape[0]
    product[...] = rounded_product(key_ref[...], value_ref[...])
    decays = spread_rows(jnp.exp(-rate), 0, modes)
    gains = spread_rows(gain_ref[...], 0, modes)

    def body(group, states):
        results = []
        for x in load_steps(product, group, steps):
            states = [d * s + x for d, s in zip(decays, states)]
            results.append(tree_sum([g * s for g, s in zip(gains, states)]))
        store_steps(conv_ref, group, steps, results)
        return states

    for n, state in enumerate(lax.fori_loop(0, steps // BLOCKS, body, zero_rows(modes))):
        ends_ref[n * BLOCKS : (n + 1) * BLOCKS, :] = state
    total_ref[0, 0] = join_blocks(ends_ref, rate, steps, False)


def backward_local_kernel(
    key_ref,
    value_ref,
    query_ref,
    grad_ref,
    rate_ref,
    gain_ref,
    forward_ends_ref,
    conv_ref,
    ends_ref,
    summary_ref,
    product,
    weighted,
    product_steps,
    weighted_steps,
    part,
    sums_ref,
):
    steps = key_ref.shape[0] // BLOCKS
    rate = rate_ref[...]
    modes = rate.shape[0]
    product[...] = rounded_product(key_ref[...], value_ref[...])
    weighted[...] = (grad_ref[...] * query_ref[...].astype(F32)).astype(BF16).astype(F32)
    decay = jnp.exp(-rate)
    groups = steps // BLOCKS

    def reorder(group, carry):
        for source, target in ((product, product_steps), (weighted, weighted_steps)):
            for inner, tile in enumerate(load_steps(source, group, steps)):
                target[step_tile(group, inner), :] = tile
        return carry

    lax.fori_loop(0, groups, reorder, 0)
    half = modes // 2
    for first in (0, half):
        decays = spread_rows(decay, first, half)
        gains = spread_rows(gain_ref[...], first, half)

        def body(outer, held, first=first, decays=decays, gains=gains):
            states, sums = held
            group = groups - 1 - outer
            results = []
            for inner in reversed(range(BLOCKS)):
                x = product_steps[step_tile(group, inner), :]
                w = weighted_steps[step_tile(group, inner), :]
                states = [d * s + w for d, s in zip(decays, states)]
                sums = [c + x * s for c, s in zip(sums, states)]
                terms = [g * s for g, s in zip(gains, states)]
                if first:
                    results.insert(0, tree_sum(terms + [part[step_tile(group, inner), :]]))
                else:
                    part[step_tile(group, inner), :] = tree_sum(terms)
            if first:
                store_steps(conv_ref, group, steps, results)
            return states, sums

        states, sums = lax.fori_loop(
            0, groups, body, (zero_rows(half), zero_rows(half))
        )
        for n in range(half):
            ends_ref[(first + n) * BLOCKS : (first + n + 1) * BLOCKS, :] = states[n]
            sums_ref[(first + n) * BLOCKS : (first + n + 1) * BLOCKS, :] = sums[n]
    step_decay = jnp.exp(-rate * float(steps))
    run = jnp.zeros((modes, LANES), F32)
    total = jnp.zeros((modes, LANES), F32)
    for b in reversed(range(BLOCKS)):
        total = total + block_rows(sums_ref, b, modes)
        total = total + decay * block_rows(forward_ends_ref, b, modes) * run
        run = run * step_decay + block_rows(ends_ref, b, modes)
    summary_ref[0, 0] = run
    summary_ref[0, 1] = total


def forward_join_kernel(row_count, held, rate_ref, answer):
    rate = rate_ref[...]
    device_decay = jnp.exp(-rate * float(row_count))
    run = jnp.zeros_like(rate)
    for e in range(held.shape[0]):
        answer[e, 0] = run
        run = run * device_decay + held[e, 0]


def backward_join_kernel(row_count, held, forward_held, rate_ref, answer):
    rate = rate_ref[...]
    count = held.shape[0]
    decay = jnp.exp(-rate)
    device_decay = jnp.exp(-rate * float(row_count))
    run = jnp.zeros_like(rate)
    total = jnp.zeros_like(rate)
    for e in reversed(range(count)):
        answer[e, 0] = run
        total = total + held[e, 1] + decay * forward_held[e, 0] * run
        run = run * device_decay + held[e, 0]
    for e in range(count):
        answer[e, 1] = total


def join(kernel, row_count, arrays, out):
    return pl.pallas_call(
        functools.partial(kernel, row_count),
        out_shape=jax.ShapeDtypeStruct(out.shape, F32),
        in_specs=[pl.BlockSpec(memory_space=pltpu.VMEM)] * len(arrays),
        out_specs=pl.BlockSpec(memory_space=pltpu.VMEM),
    )(*arrays)


def trade(chunks):
    return lax.all_to_all(chunks, "seq", split_axis=0, concat_axis=0, tiled=True)


def forward_kernel(
    query_ref,
    grad_ref,
    conv_ref,
    rate_ref,
    gain_ref,
    ends_ref,
    carry_ref,
    gated_ref,
    query_grad_ref,
    conv,
    carries,
):
    steps = query_ref.shape[0] // BLOCKS
    rate = rate_ref[...]
    modes = rate.shape[0]
    decay = jnp.exp(-rate)
    fill_carries(carry_ref[0, 0], ends_ref, rate, steps, carries, False)
    decays = spread_rows(decay, 0, modes)
    firsts = spread_rows(decay * gain_ref[...], 0, modes)

    def body(group, states):
        results = []
        for _ in range(BLOCKS):
            results.append(tree_sum(states))
            states = [d * s for d, s in zip(decays, states)]
        store_steps(conv, group, steps, results)
        return states

    starts = [g * take(carries, n) for n, g in enumerate(firsts)]
    lax.fori_loop(0, steps // BLOCKS, body, starts)
    convolved = conv_ref[...] + conv[...]
    gated_ref[...] = (query_ref[...].astype(F32) * convolved).astype(BF16)
    query_grad_ref[...] = (grad_ref[...] * convolved).astype(BF16)


def backward_kernel(
    key_ref,
    value_ref,
    conv_ref,
    rate_ref,
    gain_ref,
    ends_ref,
    carry_ref,
    key_grad_ref,
    value_grad_ref,
    conv,
    carries,
):
    steps = key_ref.shape[0] // BLOCKS
    rate = rate_ref[...]
    modes = rate.shape[0]
    decay = jnp.exp(-rate)
    fill_carries(carry_ref[0, 0], ends_ref, rate, steps, carries, True)
    decays = spread_rows(decay, 0, modes)
    firsts = spread_rows(decay * gain_ref[...], 0, modes)

    def body(outer, states):
        results = []
        for _ in range(BLOCKS):
            results.insert(0, tree_sum(states))
            states = [d * s for d, s in zip(decays, states)]
        store_steps(conv, steps // BLOCKS - 1 - outer, steps, results)
        return states

    starts = [g * take(carries, n) for n, g in enumerate(firsts)]
    lax.fori_loop(0, steps // BLOCKS, body, starts)
    grad_product = conv_ref[...] + conv[...]
    key_grad_ref[...] = (grad_product * value_ref[...].astype(F32)).astype(BF16)
    value_grad_ref[...] = (grad_product * key_ref[...].astype(F32)).astype(BF16)


def by_lanes(rows):
    return pl.BlockSpec((rows, LANES), lambda i: (0, i))


def call(kernel, arrays, specs, outs, out_specs, scratch_rows, flops):
    groups = arrays[0].shape[1] // LANES
    moved = sum(a.size * a.dtype.itemsize for a in list(arrays) + list(outs))
    return pl.pallas_call(
        kernel,
        grid=(groups,),
        in_specs=specs,
        out_specs=out_specs,
        out_shape=outs,
        scratch_shapes=[pltpu.VMEM((r, LANES), F32) for r in scratch_rows],
        cost_estimate=pl.CostEstimate(flops=flops, bytes_accessed=moved, transcendentals=0),
        compiler_params=pltpu.CompilerParams(vmem_limit_bytes=56 * 2**20),
    )(*arrays)


def to_chunks(grouped, count):
    groups, kinds, modes, lanes = grouped.shape
    cuts = count // groups
    cut = grouped.reshape(groups, kinds, cuts, modes // cuts, lanes)
    return cut.transpose(0, 2, 1, 3, 4).reshape(count, kinds, modes // cuts, lanes)


def from_chunks(chunks, groups):
    count, kinds, part, lanes = chunks.shape
    cuts = count // groups
    cut = chunks.reshape(groups, cuts, kinds, part, lanes)
    return cut.transpose(0, 2, 1, 3, 4).reshape(groups, kinds, cuts * part, lanes)


def per_device(query_in, key_in, value_in, decay_time, residue, out_weight, cotangent):
    decay_rate = 1.0 / decay_time
    norm_factor = jnp.sqrt(-jnp.expm1(-2.0 * decay_rate))
    rate = decay_rate.T
    gain = (norm_factor * residue).T
    seq_count = lax.axis_size("seq")
    rows, width = query_in.shape
    modes = rate.shape[0]
    groups = width // LANES
    work = rows * width * modes
    ends_shape = jax.ShapeDtypeStruct((modes * BLOCKS, width), F32)
    total_shape = jax.ShapeDtypeStruct((groups, 1, modes, LANES), F32)
    summary_shape = jax.ShapeDtypeStruct((groups, 2, modes, LANES), F32)
    narrow = jax.ShapeDtypeStruct((rows, width), BF16)
    wide = jax.ShapeDtypeStruct((rows, width), F32)
    big, mode_spec, ends_spec = by_lanes(rows), by_lanes(modes), by_lanes(modes * BLOCKS)
    total_spec = pl.BlockSpec((1, 1, modes, LANES), lambda i: (i, 0, 0, 0))
    summary_spec = pl.BlockSpec((1, 2, modes, LANES), lambda i: (i, 0, 0, 0))
    rate_groups = rate.reshape(modes, groups, LANES).transpose(1, 0, 2)[:, None]
    own_rate = lax.dynamic_index_in_dim(
        to_chunks(rate_groups, seq_count)[:, 0], lax.axis_index("seq"), 0, keepdims=False
    )

    all_cotangent = lax.all_gather(cotangent, "chan", axis=1, tiled=True)
    forward_local, forward_ends, forward_total = call(
        forward_local_kernel,
        (key_in, value_in, rate, gain),
        [big, big, mode_spec, mode_spec],
        [wide, ends_shape, total_shape],
        [big, ends_spec, total_spec],
        [rows],
        4 * work,
    )
    forward_held = trade(to_chunks(forward_total, seq_count))
    forward_answer = join(
        forward_join_kernel, rows, (forward_held, own_rate), forward_held
    )
    forward_carry = from_chunks(trade(forward_answer), groups)
    grad_gated = lax.dot_general(
        all_cotangent, out_weight, (((1,), (1,)), ((), ())), preferred_element_type=F32
    )
    backward_local, backward_ends, summary = call(
        backward_local_kernel,
        (key_in, value_in, query_in, grad_gated, rate, gain, forward_ends),
        [big, big, big, big, mode_spec, mode_spec, ends_spec],
        [wide, ends_shape, summary_shape],
        [big, ends_spec, summary_spec],
        [rows] * 5 + [modes * BLOCKS],
        6 * work,
    )
    backward_held = trade(to_chunks(summary, seq_count))
    backward_answer = join(
        backward_join_kernel, rows, (backward_held, forward_held, own_rate), backward_held
    )
    joined = from_chunks(trade(backward_answer), groups)
    gated, query_grad = call(
        forward_kernel,
        (query_in, grad_gated, forward_local, rate, gain, forward_ends, forward_carry),
        [big, big, big, mode_spec, mode_spec, ends_spec, total_spec],
        [narrow, narrow],
        [big, big],
        [rows, modes * BLOCKS],
        2 * work,
    )
    partial_out = jnp.dot(gated, out_weight, preferred_element_type=F32)
    mixed_out = lax.psum_scatter(
        partial_out.astype(BF16), "chan", scatter_dimension=1, tiled=True
    )
    key_grad, value_grad = call(
        backward_kernel,
        (key_in, value_in, backward_local, rate, gain, backward_ends, joined),
        [big, big, big, mode_spec, mode_spec, ends_spec, summary_spec],
        [narrow, narrow],
        [big, big],
        [rows, modes * BLOCKS],
        2 * work,
    )
    correlation = joined[:, 1].transpose(0, 2, 1).reshape(width, modes)
    residue_grad = norm_factor * correlation / jnp.sqrt(F32(rows * seq_count))
    return (mixed_out, query_grad, key_grad, value_grad, residue_grad)


def solution(mesh):
    tokens, group = P("seq", "chan"), P("chan", None)
    return jax.shard_map(
        per_device,
        mesh=mesh,
        in_specs=(tokens, tokens, tokens, group, group, group, tokens),
        out_specs=(tokens, tokens, tokens, tokens, group),
        check_vma=False,
    )
```

```python
import functools

import jax
import jax.numpy as jnp
from jax import lax
from jax.experimental import pallas as pl
from jax.experimental.pallas import tpu as pltpu
from jax.sharding import PartitionSpec as P

LANES = 128
WIDE = 256
BLOCKS = 8
F32 = jnp.float32
BF16 = jnp.bfloat16


def tree_sum(terms):
    while len(terms) > 1:
        pairs = [terms[i] + terms[i + 1] for i in range(0, len(terms) - 1, 2)]
        terms = pairs + terms[len(terms) - len(terms) % 2 :]
    return terms[0]


def swap_rows(tiles):
    rows = lax.broadcasted_iota(jnp.int32, (BLOCKS, LANES), 0)
    for bit in (1, 2, 4):
        low = (rows & bit) == 0
        swapped = list(tiles)
        for i in range(BLOCKS):
            if i & bit == 0:
                a, b = tiles[i], tiles[i | bit]
                swapped[i] = jnp.where(low, a, pltpu.roll(b, bit, axis=0))
                swapped[i | bit] = jnp.where(low, pltpu.roll(a, BLOCKS - bit, axis=0), b)
        tiles = swapped
    return tiles


def block_tile(b, group, steps):
    return pl.ds(pl.multiple_of(b * steps + group * BLOCKS, BLOCKS), BLOCKS)


def load_steps(ref, group, steps):
    return swap_rows([ref[block_tile(b, group, steps), :] for b in range(BLOCKS)])


def store_steps(ref, group, steps, tiles):
    for b, tile in enumerate(swap_rows(tiles)):
        ref[block_tile(b, group, steps), :] = tile


def step_tile(group, inner):
    return pl.ds(pl.multiple_of((group * BLOCKS + inner) * BLOCKS, BLOCKS), BLOCKS)


def spread_rows(rate, first, count):
    return [
        jnp.broadcast_to(rate[n : n + 1, :], (BLOCKS, LANES)) for n in range(first, first + count)
    ]


def block_rows(ends, b, modes):
    return ends[pl.ds(b, modes, stride=BLOCKS), :]


def join_blocks(ends, rate, steps, backward):
    modes = rate.shape[0]
    step_decay = jnp.exp(-rate * float(steps))
    total = jnp.zeros((modes, LANES), F32)
    for b in reversed(range(BLOCKS)) if backward else range(BLOCKS):
        total = total * step_decay + block_rows(ends, b, modes)
    return total


def fill_carries(entering, ends, rate, steps, carries, backward):
    modes = rate.shape[0]
    step_decay = jnp.exp(-rate * float(steps))
    run = entering
    for b in reversed(range(BLOCKS)) if backward else range(BLOCKS):
        carries[pl.ds(b, modes, stride=BLOCKS), :] = run
        run = run * step_decay + block_rows(ends, b, modes)


def take(ref, n):
    return ref[n * BLOCKS : (n + 1) * BLOCKS, :]


def rounded_product(a, b):
    return (a.astype(F32) * b.astype(F32)).astype(BF16).astype(F32)


def zero_rows(count):
    return [jnp.zeros((BLOCKS, LANES), F32) for _ in range(count)]


def forward_local_kernel(
    key_ref, value_ref, rate_ref, gain_ref, conv_ref, ends_ref, total_ref, product
):
    steps = key_ref.shape[0] // BLOCKS
    rate = rate_ref[...]
    modes = rate.shape[0]
    product[...] = rounded_product(key_ref[...], value_ref[...])
    decays = spread_rows(jnp.exp(-rate), 0, modes)
    gains = spread_rows(gain_ref[...], 0, modes)

    def body(group, states):
        results = []
        for x in load_steps(product, group, steps):
            states = [d * s + x for d, s in zip(decays, states)]
            results.append(tree_sum([g * s for g, s in zip(gains, states)]))
        store_steps(conv_ref, group, steps, results)
        return states

    for n, state in enumerate(lax.fori_loop(0, steps // BLOCKS, body, zero_rows(modes))):
        ends_ref[n * BLOCKS : (n + 1) * BLOCKS, :] = state
    total_ref[0, 0] = join_blocks(ends_ref, rate, steps, False)


def backward_local_kernel(
    key_ref,
    value_ref,
    query_ref,
    grad_ref,
    rate_ref,
    gain_ref,
    forward_ends_ref,
    forward_total_ref,
    conv_ref,
    ends_ref,
    summary_ref,
    product,
    weighted,
    product_steps,
    weighted_steps,
    part,
    sums_ref,
):
    steps = key_ref.shape[0] // BLOCKS
    rate = rate_ref[...]
    modes = rate.shape[0]
    product[...] = rounded_product(key_ref[...], value_ref[...])
    weighted[...] = (grad_ref[...] * query_ref[...].astype(F32)).astype(BF16).astype(F32)
    decay = jnp.exp(-rate)
    groups = steps // BLOCKS

    def reorder(group, carry):
        for source, target in ((product, product_steps), (weighted, weighted_steps)):
            for inner, tile in enumerate(load_steps(source, group, steps)):
                target[step_tile(group, inner), :] = tile
        return carry

    lax.fori_loop(0, groups, reorder, 0)
    half = modes // 2
    for first in (0, half):
        decays = spread_rows(decay, first, half)
        gains = spread_rows(gain_ref[...], first, half)

        def body(outer, held, first=first, decays=decays, gains=gains):
            states, sums = held
            group = groups - 1 - outer
            results = []
            for inner in reversed(range(BLOCKS)):
                x = product_steps[step_tile(group, inner), :]
                w = weighted_steps[step_tile(group, inner), :]
                states = [d * s + w for d, s in zip(decays, states)]
                sums = [c + x * s for c, s in zip(sums, states)]
                terms = [g * s for g, s in zip(gains, states)]
                if first:
                    results.insert(0, tree_sum(terms + [part[step_tile(group, inner), :]]))
                else:
                    part[step_tile(group, inner), :] = tree_sum(terms)
            if first:
                store_steps(conv_ref, group, steps, results)
            return states, sums

        states, sums = lax.fori_loop(
            0, groups, body, (zero_rows(half), zero_rows(half))
        )
        for n in range(half):
            ends_ref[(first + n) * BLOCKS : (first + n + 1) * BLOCKS, :] = states[n]
            sums_ref[(first + n) * BLOCKS : (first + n + 1) * BLOCKS, :] = sums[n]
    step_decay = jnp.exp(-rate * float(steps))
    run = jnp.zeros((modes, LANES), F32)
    total = jnp.zeros((modes, LANES), F32)
    for b in reversed(range(BLOCKS)):
        total = total + block_rows(sums_ref, b, modes)
        total = total + decay * block_rows(forward_ends_ref, b, modes) * run
        run = run * step_decay + block_rows(ends_ref, b, modes)
    summary_ref[0, 0] = forward_total_ref[0, 0]
    summary_ref[0, 1] = run
    summary_ref[0, 2] = total


def exchange_kernel(count, row_count, parts_ref, rate_ref, out_ref, held, answer, *sems):
    me = lax.axis_index("seq")
    barrier = pltpu.get_barrier_semaphore()

    def peer(k):
        return lax.rem(me + k, count)

    def source(k):
        return lax.rem(me + count - k, count)

    def greet(k, carry):
        pl.semaphore_signal(
            barrier, inc=1, device_id={"seq": peer(k)}, device_id_type=pl.DeviceIdType.MESH
        )
        return carry

    lax.fori_loop(1, count, greet, 0)
    pl.semaphore_wait(barrier, count - 1)

    def copy(k, src, dst, place, send, recv):
        return pltpu.make_async_remote_copy(
            src_ref=src.at[peer(k)],
            dst_ref=dst.at[place],
            send_sem=send.at[k],
            recv_sem=recv.at[k],
            device_id={"seq": peer(k)},
            device_id_type=pl.DeviceIdType.MESH,
        )

    def start_all(src, dst, send, recv):
        def one(k, carry):
            copy(k, src, dst, me, send, recv).start()
            return carry

        lax.fori_loop(1, count, one, 0)

    def wait_all(src, dst, send, recv):
        def one(k, carry):
            copy(k, src, dst, source(k), send, recv).wait_recv()
            return carry

        lax.fori_loop(1, count, one, 0)

    def drain_all(src, dst, send, recv):
        def one(k, carry):
            copy(k, src, dst, me, send, recv).wait_send()
            return carry

        lax.fori_loop(1, count, one, 0)

    start_all(parts_ref, held, sems[0], sems[1])
    held[me] = parts_ref[me]
    rate = rate_ref[me]
    decay = jnp.exp(-rate)
    device_decay = jnp.exp(-rate * float(row_count))
    wait_all(parts_ref, held, sems[0], sems[1])
    run = jnp.zeros_like(rate)
    for e in range(count):
        answer[e, 0] = run
        run = run * device_decay + held[e, 0]
    run = jnp.zeros_like(rate)
    total = jnp.zeros_like(rate)
    for e in reversed(range(count)):
        answer[e, 1] = run
        total = total + held[e, 2] + decay * held[e, 0] * run
        run = run * device_decay + held[e, 1]
    for e in range(count):
        answer[e, 2] = total
    start_all(answer, out_ref, sems[2], sems[3])
    out_ref[me] = answer[me]
    wait_all(answer, out_ref, sems[2], sems[3])
    drain_all(parts_ref, held, sems[0], sems[1])
    drain_all(answer, out_ref, sems[2], sems[3])


def exchange(parts, rates, row_count):
    count, kinds, modes, lanes = parts.shape
    return pl.pallas_call(
        functools.partial(exchange_kernel, count, row_count),
        out_shape=jax.ShapeDtypeStruct(parts.shape, F32),
        in_specs=[pl.BlockSpec(memory_space=pltpu.VMEM)] * 2,
        out_specs=pl.BlockSpec(memory_space=pltpu.VMEM),
        scratch_shapes=[pltpu.VMEM(parts.shape, F32)] * 2 + [pltpu.SemaphoreType.DMA((count,))] * 4,
        compiler_params=pltpu.CompilerParams(collective_id=0, has_side_effects=True),
    )(parts, rates)


def forward_kernel(
    query_ref,
    grad_ref,
    conv_ref,
    rate_ref,
    gain_ref,
    ends_ref,
    carry_ref,
    gated_ref,
    query_grad_ref,
    conv,
    carries,
):
    steps = query_ref.shape[0] // BLOCKS
    rate = rate_ref[...]
    modes = rate.shape[0]
    decay = jnp.exp(-rate)
    fill_carries(carry_ref[0, 0], ends_ref, rate, steps, carries, False)
    decays = spread_rows(decay, 0, modes)
    firsts = spread_rows(decay * gain_ref[...], 0, modes)

    def body(group, states):
        results = []
        for _ in range(BLOCKS):
            results.append(tree_sum(states))
            states = [d * s for d, s in zip(decays, states)]
        store_steps(conv, group, steps, results)
        return states

    starts = [g * take(carries, n) for n, g in enumerate(firsts)]
    lax.fori_loop(0, steps // BLOCKS, body, starts)
    convolved = conv_ref[...] + conv[...]
    gated_ref[...] = (query_ref[...].astype(F32) * convolved).astype(BF16)
    query_grad_ref[...] = (grad_ref[...] * convolved).astype(BF16)


def backward_kernel(
    key_ref,
    value_ref,
    conv_ref,
    rate_ref,
    gain_ref,
    ends_ref,
    carry_ref,
    key_grad_ref,
    value_grad_ref,
    conv,
    carries,
):
    steps = key_ref.shape[0] // BLOCKS
    rate = rate_ref[...]
    modes = rate.shape[0]
    decay = jnp.exp(-rate)
    fill_carries(carry_ref[0, 1], ends_ref, rate, steps, carries, True)
    decays = spread_rows(decay, 0, modes)
    firsts = spread_rows(decay * gain_ref[...], 0, modes)

    def body(outer, states):
        results = []
        for _ in range(BLOCKS):
            results.insert(0, tree_sum(states))
            states = [d * s for d, s in zip(decays, states)]
        store_steps(conv, steps // BLOCKS - 1 - outer, steps, results)
        return states

    starts = [g * take(carries, n) for n, g in enumerate(firsts)]
    lax.fori_loop(0, steps // BLOCKS, body, starts)
    grad_product = conv_ref[...] + conv[...]
    key_grad_ref[...] = (grad_product * value_ref[...].astype(F32)).astype(BF16)
    value_grad_ref[...] = (grad_product * key_ref[...].astype(F32)).astype(BF16)


def by_lanes(rows):
    return pl.BlockSpec((rows, WIDE), lambda i: (0, i))


def each_group(kernel, scratch_count, *refs):
    arrays, scratches = refs[: len(refs) - scratch_count], refs[len(refs) - scratch_count :]

    def one(r, i):
        if len(r.shape) == 2:
            return r.at[:, i * LANES : (i + 1) * LANES]
        return r.at[i] if len(r.shape) == 3 else r.at[i : i + 1]

    for i in range(WIDE // LANES):
        part = [one(r, i) for r in arrays]
        kernel(*part, *scratches)


def call(kernel, arrays, specs, outs, out_specs, scratch_rows, flops):
    moved = sum(a.size * a.dtype.itemsize for a in list(arrays) + list(outs))
    return pl.pallas_call(
        functools.partial(each_group, kernel, len(scratch_rows)),
        grid=(arrays[0].shape[1] // WIDE,),
        in_specs=specs,
        out_specs=out_specs,
        out_shape=outs,
        scratch_shapes=[pltpu.VMEM((r, LANES), F32) for r in scratch_rows],
        cost_estimate=pl.CostEstimate(flops=flops, bytes_accessed=moved, transcendentals=0),
        compiler_params=pltpu.CompilerParams(vmem_limit_bytes=56 * 2**20),
    )(*arrays)


def to_chunks(grouped, count):
    groups, kinds, modes, lanes = grouped.shape
    cuts = count // groups
    cut = grouped.reshape(groups, kinds, cuts, modes // cuts, lanes)
    return cut.transpose(0, 2, 1, 3, 4).reshape(count, kinds, modes // cuts, lanes)


def from_chunks(chunks, groups):
    count, kinds, part, lanes = chunks.shape
    cuts = count // groups
    cut = chunks.reshape(groups, cuts, kinds, part, lanes)
    return cut.transpose(0, 2, 1, 3, 4).reshape(groups, kinds, cuts * part, lanes)


def per_device(query_in, key_in, value_in, decay_time, residue, out_weight, cotangent):
    decay_rate = 1.0 / decay_time
    norm_factor = jnp.sqrt(-jnp.expm1(-2.0 * decay_rate))
    rate = decay_rate.T
    gain = (norm_factor * residue).T
    seq_count = lax.axis_size("seq")
    rows, width = query_in.shape
    modes = rate.shape[0]
    groups = width // LANES
    work = rows * width * modes
    wide_groups = WIDE // LANES
    ends_shape = jax.ShapeDtypeStruct((groups, modes * BLOCKS, LANES), F32)
    total_shape = jax.ShapeDtypeStruct((groups, 1, modes, LANES), F32)
    summary_shape = jax.ShapeDtypeStruct((groups, 3, modes, LANES), F32)
    narrow = jax.ShapeDtypeStruct((rows, width), BF16)
    wide = jax.ShapeDtypeStruct((rows, width), F32)
    big, mode_spec = by_lanes(rows), by_lanes(modes)
    ends_spec = pl.BlockSpec((wide_groups, modes * BLOCKS, LANES), lambda i: (i, 0, 0))
    total_spec = pl.BlockSpec((wide_groups, 1, modes, LANES), lambda i: (i, 0, 0, 0))
    summary_spec = pl.BlockSpec((wide_groups, 3, modes, LANES), lambda i: (i, 0, 0, 0))
    rate_groups = rate.reshape(modes, groups, LANES).transpose(1, 0, 2)[:, None]
    all_cotangent = lax.all_gather(cotangent, "chan", axis=1, tiled=True)
    forward_local, forward_ends, forward_total = call(
        forward_local_kernel,
        (key_in, value_in, rate, gain),
        [big, big, mode_spec, mode_spec],
        [wide, ends_shape, total_shape],
        [big, ends_spec, total_spec],
        [rows],
        4 * work,
    )
    grad_gated = lax.dot_general(
        all_cotangent, out_weight, (((1,), (1,)), ((), ())), preferred_element_type=F32
    )
    backward_local, backward_ends, summary = call(
        backward_local_kernel,
        (key_in, value_in, query_in, grad_gated, rate, gain, forward_ends, forward_total),
        [big, big, big, big, mode_spec, mode_spec, ends_spec, total_spec],
        [wide, ends_shape, summary_shape],
        [big, ends_spec, summary_spec],
        [rows] * 5 + [modes * BLOCKS],
        6 * work,
    )
    joined = from_chunks(
        exchange(to_chunks(summary, seq_count), to_chunks(rate_groups, seq_count)[:, 0], rows),
        groups,
    )
    gated, query_grad = call(
        forward_kernel,
        (query_in, grad_gated, forward_local, rate, gain, forward_ends, joined),
        [big, big, big, mode_spec, mode_spec, ends_spec, summary_spec],
        [narrow, narrow],
        [big, big],
        [rows, modes * BLOCKS],
        2 * work,
    )
    partial_out = jnp.dot(gated, out_weight, preferred_element_type=F32)
    mixed_out = lax.psum_scatter(
        partial_out.astype(BF16), "chan", scatter_dimension=1, tiled=True
    )
    key_grad, value_grad = call(
        backward_kernel,
        (key_in, value_in, backward_local, rate, gain, backward_ends, joined),
        [big, big, big, mode_spec, mode_spec, ends_spec, summary_spec],
        [narrow, narrow],
        [big, big],
        [rows, modes * BLOCKS],
        2 * work,
    )
    correlation = joined[:, 2].transpose(0, 2, 1).reshape(width, modes)
    residue_grad = norm_factor * correlation / jnp.sqrt(F32(rows * seq_count))
    return (mixed_out, query_grad, key_grad, value_grad, residue_grad)


def solution(mesh):
    tokens, group = P("seq", "chan"), P("chan", None)
    return jax.shard_map(
        per_device,
        mesh=mesh,
        in_specs=(tokens, tokens, tokens, group, group, group, tokens),
        out_specs=(tokens, tokens, tokens, tokens, group),
        check_vma=False,
    )
```

```python
import functools

import jax
import jax.numpy as jnp
from jax import lax
from jax.experimental import pallas as pl
from jax.experimental.pallas import tpu as pltpu
from jax.sharding import PartitionSpec as P

LANES = 128
WIDE = 512
BLOCKS = 8
F32 = jnp.float32
BF16 = jnp.bfloat16


def tree_sum(terms):
    while len(terms) > 1:
        pairs = [terms[i] + terms[i + 1] for i in range(0, len(terms) - 1, 2)]
        terms = pairs + terms[len(terms) - len(terms) % 2 :]
    return terms[0]


def swap_rows(tiles):
    rows = lax.broadcasted_iota(jnp.int32, (BLOCKS, LANES), 0)
    for bit in (1, 2, 4):
        low = (rows & bit) == 0
        swapped = list(tiles)
        for i in range(BLOCKS):
            if i & bit == 0:
                a, b = tiles[i], tiles[i | bit]
                swapped[i] = jnp.where(low, a, pltpu.roll(b, bit, axis=0))
                swapped[i | bit] = jnp.where(low, pltpu.roll(a, BLOCKS - bit, axis=0), b)
        tiles = swapped
    return tiles


def block_tile(b, group, steps):
    return pl.ds(pl.multiple_of(b * steps + group * BLOCKS, BLOCKS), BLOCKS)


def load_steps(ref, group, steps):
    return swap_rows([ref[block_tile(b, group, steps), :] for b in range(BLOCKS)])


def store_steps(ref, group, steps, tiles):
    for b, tile in enumerate(swap_rows(tiles)):
        ref[block_tile(b, group, steps), :] = tile


def step_tile(group, inner):
    return pl.ds(pl.multiple_of((group * BLOCKS + inner) * BLOCKS, BLOCKS), BLOCKS)


def spread_rows(rate, first, count):
    return [
        jnp.broadcast_to(rate[n : n + 1, :], (BLOCKS, LANES)) for n in range(first, first + count)
    ]


def block_rows(ends, b, modes):
    return ends[pl.ds(b, modes, stride=BLOCKS), :]


def join_blocks(ends, rate, steps, backward):
    modes = rate.shape[0]
    step_decay = jnp.exp(-rate * float(steps))
    total = jnp.zeros((modes, LANES), F32)
    for b in reversed(range(BLOCKS)) if backward else range(BLOCKS):
        total = total * step_decay + block_rows(ends, b, modes)
    return total


def fill_carries(entering, ends, rate, steps, carries, backward):
    modes = rate.shape[0]
    step_decay = jnp.exp(-rate * float(steps))
    run = entering
    for b in reversed(range(BLOCKS)) if backward else range(BLOCKS):
        carries[pl.ds(b, modes, stride=BLOCKS), :] = run
        run = run * step_decay + block_rows(ends, b, modes)


def take(ref, n):
    return ref[n * BLOCKS : (n + 1) * BLOCKS, :]


def rounded_product(a, b):
    return (a.astype(F32) * b.astype(F32)).astype(BF16).astype(F32)


def zero_rows(count):
    return [jnp.zeros((BLOCKS, LANES), F32) for _ in range(count)]


def forward_local_kernel(
    key_ref, value_ref, rate_ref, gain_ref, conv_ref, ends_ref, total_ref, product
):
    steps = key_ref.shape[0] // BLOCKS
    rate = rate_ref[...]
    modes = rate.shape[0]
    product[...] = rounded_product(key_ref[...], value_ref[...])
    decays = spread_rows(jnp.exp(-rate), 0, modes)
    gains = spread_rows(gain_ref[...], 0, modes)

    def body(group, states):
        results = []
        for x in load_steps(product, group, steps):
            states = [d * s + x for d, s in zip(decays, states)]
            results.append(tree_sum([g * s for g, s in zip(gains, states)]))
        store_steps(conv_ref, group, steps, results)
        return states

    for n, state in enumerate(lax.fori_loop(0, steps // BLOCKS, body, zero_rows(modes))):
        ends_ref[n * BLOCKS : (n + 1) * BLOCKS, :] = state
    total_ref[0, 0] = join_blocks(ends_ref, rate, steps, False)


def backward_local_kernel(
    key_ref,
    value_ref,
    query_ref,
    grad_ref,
    rate_ref,
    gain_ref,
    forward_ends_ref,
    forward_total_ref,
    conv_ref,
    ends_ref,
    summary_ref,
    product,
    weighted,
    product_steps,
    weighted_steps,
    part,
    sums_ref,
):
    steps = key_ref.shape[0] // BLOCKS
    rate = rate_ref[...]
    modes = rate.shape[0]
    product[...] = rounded_product(key_ref[...], value_ref[...])
    weighted[...] = (grad_ref[...] * query_ref[...].astype(F32)).astype(BF16).astype(F32)
    decay = jnp.exp(-rate)
    groups = steps // BLOCKS

    def reorder(group, carry):
        for source, target in ((product, product_steps), (weighted, weighted_steps)):
            for inner, tile in enumerate(load_steps(source, group, steps)):
                target[step_tile(group, inner), :] = tile
        return carry

    lax.fori_loop(0, groups, reorder, 0)
    half = modes // 2
    for first in (0, half):
        decays = spread_rows(decay, first, half)
        gains = spread_rows(gain_ref[...], first, half)

        def body(outer, held, first=first, decays=decays, gains=gains):
            states, sums = held
            group = groups - 1 - outer
            results = []
            for inner in reversed(range(BLOCKS)):
                x = product_steps[step_tile(group, inner), :]
                w = weighted_steps[step_tile(group, inner), :]
                states = [d * s + w for d, s in zip(decays, states)]
                sums = [c + x * s for c, s in zip(sums, states)]
                terms = [g * s for g, s in zip(gains, states)]
                if first:
                    results.insert(0, tree_sum(terms + [part[step_tile(group, inner), :]]))
                else:
                    part[step_tile(group, inner), :] = tree_sum(terms)
            if first:
                store_steps(conv_ref, group, steps, results)
            return states, sums

        states, sums = lax.fori_loop(
            0, groups, body, (zero_rows(half), zero_rows(half))
        )
        for n in range(half):
            ends_ref[(first + n) * BLOCKS : (first + n + 1) * BLOCKS, :] = states[n]
            sums_ref[(first + n) * BLOCKS : (first + n + 1) * BLOCKS, :] = sums[n]
    step_decay = jnp.exp(-rate * float(steps))
    run = jnp.zeros((modes, LANES), F32)
    total = jnp.zeros((modes, LANES), F32)
    for b in reversed(range(BLOCKS)):
        total = total + block_rows(sums_ref, b, modes)
        total = total + decay * block_rows(forward_ends_ref, b, modes) * run
        run = run * step_decay + block_rows(ends_ref, b, modes)
    summary_ref[0, 0] = forward_total_ref[0, 0]
    summary_ref[0, 1] = run
    summary_ref[0, 2] = total


def exchange_kernel(count, row_count, parts_ref, rate_ref, out_ref, held, answer, *sems):
    me = lax.axis_index("seq")
    barrier = pltpu.get_barrier_semaphore()

    def peer(k):
        return lax.rem(me + k, count)

    def source(k):
        return lax.rem(me + count - k, count)

    def greet(k, carry):
        pl.semaphore_signal(
            barrier, inc=1, device_id={"seq": peer(k)}, device_id_type=pl.DeviceIdType.MESH
        )
        return carry

    lax.fori_loop(1, count, greet, 0)
    pl.semaphore_wait(barrier, count - 1)

    def copy(k, src, dst, place, send, recv):
        return pltpu.make_async_remote_copy(
            src_ref=src.at[peer(k)],
            dst_ref=dst.at[place],
            send_sem=send.at[k],
            recv_sem=recv.at[k],
            device_id={"seq": peer(k)},
            device_id_type=pl.DeviceIdType.MESH,
        )

    def start_all(src, dst, send, recv):
        def one(k, carry):
            copy(k, src, dst, me, send, recv).start()
            return carry

        lax.fori_loop(1, count, one, 0)

    def wait_all(src, dst, send, recv):
        def one(k, carry):
            copy(k, src, dst, source(k), send, recv).wait_recv()
            return carry

        lax.fori_loop(1, count, one, 0)

    def drain_all(src, dst, send, recv):
        def one(k, carry):
            copy(k, src, dst, me, send, recv).wait_send()
            return carry

        lax.fori_loop(1, count, one, 0)

    start_all(parts_ref, held, sems[0], sems[1])
    held[me] = parts_ref[me]
    rate = rate_ref[me]
    decay = jnp.exp(-rate)
    device_decay = jnp.exp(-rate * float(row_count))
    wait_all(parts_ref, held, sems[0], sems[1])
    run = jnp.zeros_like(rate)
    for e in range(count):
        answer[e, 0] = run
        run = run * device_decay + held[e, 0]
    run = jnp.zeros_like(rate)
    total = jnp.zeros_like(rate)
    for e in reversed(range(count)):
        answer[e, 1] = run
        total = total + held[e, 2] + decay * held[e, 0] * run
        run = run * device_decay + held[e, 1]
    for e in range(count):
        answer[e, 2] = total
    start_all(answer, out_ref, sems[2], sems[3])
    out_ref[me] = answer[me]
    wait_all(answer, out_ref, sems[2], sems[3])
    drain_all(parts_ref, held, sems[0], sems[1])
    drain_all(answer, out_ref, sems[2], sems[3])


def exchange(parts, rates, row_count):
    count, kinds, modes, lanes = parts.shape
    return pl.pallas_call(
        functools.partial(exchange_kernel, count, row_count),
        out_shape=jax.ShapeDtypeStruct(parts.shape, F32),
        in_specs=[pl.BlockSpec(memory_space=pltpu.VMEM)] * 2,
        out_specs=pl.BlockSpec(memory_space=pltpu.VMEM),
        scratch_shapes=[pltpu.VMEM(parts.shape, F32)] * 2 + [pltpu.SemaphoreType.DMA((count,))] * 4,
        compiler_params=pltpu.CompilerParams(collective_id=0, has_side_effects=True),
    )(parts, rates)


def forward_kernel(
    query_ref,
    grad_ref,
    conv_ref,
    rate_ref,
    gain_ref,
    ends_ref,
    carry_ref,
    gated_ref,
    query_grad_ref,
    conv,
    carries,
):
    steps = query_ref.shape[0] // BLOCKS
    rate = rate_ref[...]
    modes = rate.shape[0]
    decay = jnp.exp(-rate)
    fill_carries(carry_ref[0, 0], ends_ref, rate, steps, carries, False)
    decays = spread_rows(decay, 0, modes)
    firsts = spread_rows(decay * gain_ref[...], 0, modes)

    def body(group, states):
        results = []
        for _ in range(BLOCKS):
            results.append(tree_sum(states))
            states = [d * s for d, s in zip(decays, states)]
        store_steps(conv, group, steps, results)
        return states

    starts = [g * take(carries, n) for n, g in enumerate(firsts)]
    lax.fori_loop(0, steps // BLOCKS, body, starts)
    convolved = conv_ref[...] + conv[...]
    gated_ref[...] = (query_ref[...].astype(F32) * convolved).astype(BF16)
    query_grad_ref[...] = (grad_ref[...] * convolved).astype(BF16)


def backward_kernel(
    key_ref,
    value_ref,
    conv_ref,
    rate_ref,
    gain_ref,
    ends_ref,
    carry_ref,
    key_grad_ref,
    value_grad_ref,
    conv,
    carries,
):
    steps = key_ref.shape[0] // BLOCKS
    rate = rate_ref[...]
    modes = rate.shape[0]
    decay = jnp.exp(-rate)
    fill_carries(carry_ref[0, 1], ends_ref, rate, steps, carries, True)
    decays = spread_rows(decay, 0, modes)
    firsts = spread_rows(decay * gain_ref[...], 0, modes)

    def body(outer, states):
        results = []
        for _ in range(BLOCKS):
            results.insert(0, tree_sum(states))
            states = [d * s for d, s in zip(decays, states)]
        store_steps(conv, steps // BLOCKS - 1 - outer, steps, results)
        return states

    starts = [g * take(carries, n) for n, g in enumerate(firsts)]
    lax.fori_loop(0, steps // BLOCKS, body, starts)
    grad_product = conv_ref[...] + conv[...]
    key_grad_ref[...] = (grad_product * value_ref[...].astype(F32)).astype(BF16)
    value_grad_ref[...] = (grad_product * key_ref[...].astype(F32)).astype(BF16)


def by_lanes(rows):
    return pl.BlockSpec((rows, WIDE), lambda i: (0, i))


def each_group(kernel, scratch_count, *refs):
    arrays, scratches = refs[: len(refs) - scratch_count], refs[len(refs) - scratch_count :]

    def one(r, i):
        if len(r.shape) == 2:
            return r.at[:, i * LANES : (i + 1) * LANES]
        return r.at[i] if len(r.shape) == 3 else r.at[i : i + 1]

    for i in range(WIDE // LANES):
        part = [one(r, i) for r in arrays]
        kernel(*part, *scratches)


def call(kernel, arrays, specs, outs, out_specs, scratch_rows, flops):
    moved = sum(a.size * a.dtype.itemsize for a in list(arrays) + list(outs))
    return pl.pallas_call(
        functools.partial(each_group, kernel, len(scratch_rows)),
        grid=(arrays[0].shape[1] // WIDE,),
        in_specs=specs,
        out_specs=out_specs,
        out_shape=outs,
        scratch_shapes=[pltpu.VMEM((r, LANES), F32) for r in scratch_rows],
        cost_estimate=pl.CostEstimate(flops=flops, bytes_accessed=moved, transcendentals=0),
        compiler_params=pltpu.CompilerParams(vmem_limit_bytes=56 * 2**20),
    )(*arrays)


def to_chunks(grouped, count):
    groups, kinds, modes, lanes = grouped.shape
    cuts = count // groups
    cut = grouped.reshape(groups, kinds, cuts, modes // cuts, lanes)
    return cut.transpose(0, 2, 1, 3, 4).reshape(count, kinds, modes // cuts, lanes)


def from_chunks(chunks, groups):
    count, kinds, part, lanes = chunks.shape
    cuts = count // groups
    cut = chunks.reshape(groups, cuts, kinds, part, lanes)
    return cut.transpose(0, 2, 1, 3, 4).reshape(groups, kinds, cuts * part, lanes)


def per_device(query_in, key_in, value_in, decay_time, residue, out_weight, cotangent):
    decay_rate = 1.0 / decay_time
    norm_factor = jnp.sqrt(-jnp.expm1(-2.0 * decay_rate))
    rate = decay_rate.T
    gain = (norm_factor * residue).T
    seq_count = lax.axis_size("seq")
    rows, width = query_in.shape
    modes = rate.shape[0]
    groups = width // LANES
    work = rows * width * modes
    wide_groups = WIDE // LANES
    ends_shape = jax.ShapeDtypeStruct((groups, modes * BLOCKS, LANES), F32)
    total_shape = jax.ShapeDtypeStruct((groups, 1, modes, LANES), F32)
    summary_shape = jax.ShapeDtypeStruct((groups, 3, modes, LANES), F32)
    narrow = jax.ShapeDtypeStruct((rows, width), BF16)
    wide = jax.ShapeDtypeStruct((rows, width), F32)
    big, mode_spec = by_lanes(rows), by_lanes(modes)
    ends_spec = pl.BlockSpec((wide_groups, modes * BLOCKS, LANES), lambda i: (i, 0, 0))
    total_spec = pl.BlockSpec((wide_groups, 1, modes, LANES), lambda i: (i, 0, 0, 0))
    summary_spec = pl.BlockSpec((wide_groups, 3, modes, LANES), lambda i: (i, 0, 0, 0))
    rate_groups = rate.reshape(modes, groups, LANES).transpose(1, 0, 2)[:, None]
    all_cotangent = lax.all_gather(cotangent, "chan", axis=1, tiled=True)
    forward_local, forward_ends, forward_total = call(
        forward_local_kernel,
        (key_in, value_in, rate, gain),
        [big, big, mode_spec, mode_spec],
        [wide, ends_shape, total_shape],
        [big, ends_spec, total_spec],
        [rows],
        4 * work,
    )
    grad_gated = lax.dot_general(
        all_cotangent, out_weight, (((1,), (1,)), ((), ())), preferred_element_type=F32
    )
    backward_local, backward_ends, summary = call(
        backward_local_kernel,
        (key_in, value_in, query_in, grad_gated, rate, gain, forward_ends, forward_total),
        [big, big, big, big, mode_spec, mode_spec, ends_spec, total_spec],
        [wide, ends_shape, summary_shape],
        [big, ends_spec, summary_spec],
        [rows] * 5 + [modes * BLOCKS],
        6 * work,
    )
    joined = from_chunks(
        exchange(to_chunks(summary, seq_count), to_chunks(rate_groups, seq_count)[:, 0], rows),
        groups,
    )
    gated, query_grad = call(
        forward_kernel,
        (query_in, grad_gated, forward_local, rate, gain, forward_ends, joined),
        [big, big, big, mode_spec, mode_spec, ends_spec, summary_spec],
        [narrow, narrow],
        [big, big],
        [rows, modes * BLOCKS],
        2 * work,
    )
    partial_out = jnp.dot(gated, out_weight, preferred_element_type=F32)
    mixed_out = lax.psum_scatter(
        partial_out.astype(BF16), "chan", scatter_dimension=1, tiled=True
    )
    key_grad, value_grad = call(
        backward_kernel,
        (key_in, value_in, backward_local, rate, gain, backward_ends, joined),
        [big, big, big, mode_spec, mode_spec, ends_spec, summary_spec],
        [narrow, narrow],
        [big, big],
        [rows, modes * BLOCKS],
        2 * work,
    )
    correlation = joined[:, 2].transpose(0, 2, 1).reshape(width, modes)
    residue_grad = norm_factor * correlation / jnp.sqrt(F32(rows * seq_count))
    return (mixed_out, query_grad, key_grad, value_grad, residue_grad)


def solution(mesh):
    tokens, group = P("seq", "chan"), P("chan", None)
    return jax.shard_map(
        per_device,
        mesh=mesh,
        in_specs=(tokens, tokens, tokens, group, group, group, tokens),
        out_specs=(tokens, tokens, tokens, tokens, group),
        check_vma=False,
    )
```
